32 devices in a mesh: dp: 4 (over y, core), expert: 4 (over z), section: 2 (over x).
Axes of the slice: x: 2, y: 2, z: 4, core: 2. Of those that a mesh axis runs over, the one named last changes fastest.
Arguments:
- inputs: bfloat16 [2, 2048, 2048], P('section', ('dp', 'expert')), may hold values from -6 to 6
- out_grad: bfloat16 [2, 2048, 2048], P('section', ('dp', 'expert')), may hold values from -6 to 6
- expert_ids: int32 [2, 2048, 4], P('section', ('dp', 'expert')), may hold values from 0 to 7, all different within a row; in each aligned block of 128 rows (0 to 127, 128 to 255, ..., all dimensions but the last counted through in order) at most 72 rows name the same one
- gate_weights: float32 [2, 2048, 4], P('section', ('dp', 'expert')), may hold values from 0.05 to 0.6
- w_gate: bfloat16 [2, 8, 768, 2048], P('section', 'expert', 'dp'), may hold values from -0.125 to 0.125
- w_up: bfloat16 [2, 8, 768, 2048], P('section', 'expert', 'dp'), may hold values from -0.125 to 0.125
- w_down: bfloat16 [2, 8, 768, 2048], P('section', 'expert', 'dp'), may hold values from -0.21875 to 0.21875
Outputs:
- grad_prev: bfloat16 [2, 2048, 2048], P('section', ('dp', 'expert'))
- grad_gate: bfloat16 [2, 8, 768, 2048], P('section', 'expert', 'dp')
- grad_up: bfloat16 [2, 8, 768, 2048], P('section', 'expert', 'dp')
- grad_down: bfloat16 [2, 8, 768, 2048], P('section', 'expert', 'dp')
The draws below stay inside these ranges and needn't reach their ends.
Inputs may be any that keep to these rules, and one draw needn't show every extreme that they name: `expert_ids`: each row names 4 different experts. In the rows of one device no expert is named by more than 72 rows, and in some devices' rows one expert is named by exactly 72.
All inputs are finite; a program needn't handle non-finite values.
Results may differ from the reference program's by a relative error of at most 0.013.
Values may be sent and summed in bfloat16 or wider, within the bound.
A program may use at most 192 MiB of HBM per device.

```python
import math
import jax
import jax.numpy as jnp
import numpy as np
from jax import lax

D = 2048
H = 768
TOP = 4
TOK_DEV = 128
EXPERTS = 8
CAP = 72
HS = 192
TOKENS = 2048
SECTIONS = 2
N_DP = 4
N_EXPERT = 4


def levels(rng, extent, cuts, smallest, high):
    factor_of = 1.0
    for dim, blocks in cuts:
        draws = jax.random.uniform(jax.random.fold_in(jax.random.fold_in(rng, 6), dim), (blocks,), jnp.float32, smallest / len(cuts), high / len(cuts))
        factor_of = factor_of * jnp.repeat(jnp.exp(draws), extent[dim] // blocks).reshape((-1,) + (1,) * (len(extent) - 1 - dim))
    return factor_of


def shared_out(key, own, number, rows, amount, top, limit, slope):
    ranking = jax.random.permutation(key, amount)
    crowded, ordinary = load_shares(amount, rows * top, limit, slope, True), load_shares(amount, rows * top, limit, slope, False)
    places = jnp.arange(amount)

    def named(sizes, offset_by):
        used = int((sizes > 0).sum())
        fixed = max(1, used // 4)
        passed = fixed + (places - fixed + offset_by * (used - fixed)) % max(1, amount - fixed)
        return jnp.zeros((amount,), jnp.int32).at[ranking[jnp.where(places < fixed, places, passed)]].set(jnp.asarray(sizes, jnp.int32))

    sizes = jnp.where(number % 4 == 0, named(crowded, number // 4), named(ordinary, number - number // 4 - 1))
    mixed = jax.random.permutation(jax.random.fold_in(own, 3), amount)
    giver, sink = mixed[0:amount // 2 * 2:2], mixed[1:amount // 2 * 2:2]
    margin = jnp.minimum(sizes[giver] - 1, limit - sizes[sink]) // 2
    margin = jnp.where((giver == ranking[0]) | (sink == ranking[0]) | (sizes[sink] == 0), 0, jnp.maximum(margin, 0))
    passed = jax.random.randint(jax.random.fold_in(own, 4), (amount // 2,), 0, 1 << 20) % (margin + 1)
    sizes = sizes.at[giver].add(-passed).at[sink].add(passed)
    items = jnp.searchsorted(jnp.cumsum(sizes), jnp.arange(rows * top), side="right").astype(jnp.int32)
    table = items.reshape(top, rows).T
    table = table[jax.random.permutation(jax.random.fold_in(own, 1), rows)]
    offset_by = jax.random.randint(jax.random.fold_in(own, 2), (rows, 1), 0, top)
    return jnp.take_along_axis(table, (jnp.arange(top)[None, :] + offset_by) % top, axis=1)


def load_shares(amount, total, most, skew, full):
    portions = [(1 << 20) // math.isqrt(standing ** skew) + 1 for standing in range(1, amount + 1)]
    largest = most if full else min(most, max(-(-total // amount), total * portions[0] // sum(portions)))
    least = 1 if total - largest >= amount - 1 else 0
    holding, spare = [largest] + [least] * (amount - 1), total - largest - least * (amount - 1)
    while spare > 0:
        candidates = [i for i in range(1, amount) if holding[i] < largest] or [i for i in range(1, amount) if holding[i] < most]
        pool, budget = sum([portions[i] for i in candidates]), spare
        for i in candidates:
            more = min(most - holding[i], max(1, budget * portions[i] // pool), spare)
            holding[i] = holding[i] + more
            spare = spare - more
    return np.array(holding)


def noise(key, extent, deviation, bound, pieces=(), held_as=jnp.bfloat16):
    entries = deviation * jax.random.normal(key, extent, jnp.float32)
    if pieces:
        entries = entries * levels(key, extent, pieces, -0.22, 0.18)
    return jnp.clip(entries, -bound, bound).astype(held_as)


def setup_inputs(seed: int = 0) -> dict:
    splits = jax.random.split(jax.random.key(seed), 8)
    inputs = noise(splits[0], (SECTIONS, TOKENS, D), 1.0, 6.0, ((0, 2), (1, 16)))
    out_grad = noise(splits[1], (SECTIONS, TOKENS, D), 1.0, 6.0, ((0, 2), (1, 16)))
    expert_ids_keys = jax.random.split(jax.random.fold_in(splits[2], 1), SECTIONS * TOKENS // TOK_DEV)
    expert_ids_turns = jax.random.permutation(jax.random.fold_in(splits[2], 3), SECTIONS * TOKENS // TOK_DEV)
    expert_ids = jax.vmap(lambda own, number: shared_out(jax.random.fold_in(splits[2], 2), own, number, TOK_DEV, EXPERTS, TOP, CAP, 2))(expert_ids_keys, expert_ids_turns).reshape((SECTIONS, TOKENS, TOP))
    gate_weights = jnp.clip(jnp.exp(math.log(0.6) - 2.4849067 * jax.random.uniform(splits[3], (SECTIONS, TOKENS, TOP), jnp.float32) ** levels(splits[3], (SECTIONS, TOKENS, TOP), ((0, 2), (1, 16)), -0.2, 0.2)), 0.05, 0.6)
    w_gate = noise(splits[4], (SECTIONS, EXPERTS, H, D), D ** -0.5, 0.125, ((0, 2), (1, 4), (2, 4)))
    w_up = noise(splits[5], (SECTIONS, EXPERTS, H, D), D ** -0.5, 0.125, ((0, 2), (1, 4), (2, 4)))
    w_down = noise(splits[6], (SECTIONS, EXPERTS, H, D), H ** -0.5, 0.21875, ((0, 2), (1, 4), (2, 4)))
    return {"inputs": inputs, "out_grad": out_grad, "expert_ids": expert_ids, "gate_weights": gate_weights, "w_gate": w_gate, "w_up": w_up, "w_down": w_down}


def slot_index(block_ids):
    flat_ids = block_ids.reshape(-1).astype(jnp.int32)
    onehot = (flat_ids[:, None] == jnp.arange(EXPERTS, dtype=jnp.int32)[None, :]).astype(jnp.int32)
    before = jnp.cumsum(onehot, axis=0) - onehot
    return (flat_ids * CAP + jnp.sum(before * onehot, axis=1)).astype(jnp.int32)


def expert_pass(packed):
    rows_in, rows_grad, gate_mat, up_mat, down_mat = packed
    pre_gate = jnp.dot(rows_in, gate_mat.T, preferred_element_type=jnp.float32)
    pre_up = jnp.dot(rows_in, up_mat.T, preferred_element_type=jnp.float32)
    sigmoid_gate = jax.nn.sigmoid(pre_gate)
    act_gate = pre_gate * sigmoid_gate
    hidden = (act_gate * pre_up).astype(jnp.bfloat16)
    hidden_grad = jnp.dot(rows_grad, down_mat.T, preferred_element_type=jnp.float32)
    gate_delta = (hidden_grad * pre_up * sigmoid_gate * (1.0 + pre_gate * (1.0 - sigmoid_gate))).astype(jnp.bfloat16)
    up_delta = (hidden_grad * act_gate).astype(jnp.bfloat16)
    grad_gate = jnp.dot(gate_delta.T, rows_in, preferred_element_type=jnp.float32).astype(jnp.bfloat16)
    grad_up = jnp.dot(up_delta.T, rows_in, preferred_element_type=jnp.float32).astype(jnp.bfloat16)
    grad_down = jnp.dot(hidden.T, rows_grad, preferred_element_type=jnp.float32).astype(jnp.bfloat16)
    count = rows_in.shape[0]
    part = jnp.einsum("rqh,qhd->qrd", gate_delta.astype(jnp.float32).reshape(count, N_DP, HS),
                      gate_mat.astype(jnp.float32).reshape(N_DP, HS, D))
    part = part + jnp.einsum("rqh,qhd->qrd", up_delta.astype(jnp.float32).reshape(count, N_DP, HS),
                             up_mat.astype(jnp.float32).reshape(N_DP, HS, D))
    row_grad = part.astype(jnp.bfloat16).astype(jnp.float32).sum(axis=0).astype(jnp.bfloat16)
    return grad_gate, grad_up, grad_down, row_grad


def section_pass(tokens, grads_out, route_ids, gates, gate_w, up_w, down_w):
    sources = N_DP * N_EXPERT
    slots = jax.vmap(slot_index)(route_ids.reshape(sources, TOK_DEV, TOP))
    rows_in = jnp.repeat(tokens.reshape(sources, TOK_DEV, D), TOP, axis=1)
    scaled = (gates.reshape(sources, TOK_DEV, TOP, 1).astype(jnp.float32)
              * grads_out.reshape(sources, TOK_DEV, 1, D).astype(jnp.float32)).astype(jnp.bfloat16)
    scaled = scaled.reshape(sources, TOK_DEV * TOP, D)
    anchor = jnp.broadcast_to(jnp.arange(sources, dtype=jnp.int32)[:, None], slots.shape)
    buffer_in = jnp.zeros((sources, EXPERTS * CAP, D), jnp.bfloat16).at[anchor, slots].set(rows_in)
    buffer_grad = jnp.zeros((sources, EXPERTS * CAP, D), jnp.bfloat16).at[anchor, slots].set(scaled)

    def regroup(buffer):
        return buffer.reshape(sources, EXPERTS, CAP, D).transpose(1, 0, 2, 3).reshape(EXPERTS, sources * CAP, D)

    grad_gate, grad_up, grad_down, row_grad = lax.map(
        expert_pass, (regroup(buffer_in), regroup(buffer_grad), gate_w, up_w, down_w))
    back = row_grad.reshape(EXPERTS, sources, CAP, D).transpose(1, 0, 2, 3).reshape(sources, EXPERTS * CAP, D)
    picked = jnp.take_along_axis(back, slots[:, :, None], axis=1)
    token_grad = picked.astype(jnp.float32).reshape(sources, TOK_DEV, TOP, D).sum(axis=2)
    token_grad = token_grad.astype(jnp.bfloat16).reshape(TOKENS, D)
    return token_grad, grad_gate, grad_up, grad_down


def reference(inputs, out_grad, expert_ids, gate_weights, w_gate, w_up, w_down):
    token_list = []
    gate_list = []
    up_list = []
    down_list = []
    for section_number in range(SECTIONS):
        token_grad, grad_gate, grad_up, grad_down = section_pass(
            inputs[section_number], out_grad[section_number], expert_ids[section_number],
            gate_weights[section_number], w_gate[section_number], w_up[section_number], w_down[section_number])
        token_list.append(token_grad)
        gate_list.append(grad_gate)
        up_list.append(grad_up)
        down_list.append(grad_down)
    grad_prev = jnp.stack(token_list[1:] + [jnp.zeros_like(token_list[0])])
    return grad_prev, jnp.stack(gate_list), jnp.stack(up_list), jnp.stack(down_list)
```

```python
import jax
import jax.numpy as jnp
from jax import lax
from jax.sharding import PartitionSpec as P

GROUP = ("dp", "expert")


def passed_along(block, axis, distance):
    devices = range(lax.axis_size(axis))
    route = [(i - distance, i) for i in devices if i - distance in devices]
    return lax.ppermute(block, axis, route)


def rows_by(a, b):
    return lax.dot_general(a, b, (((1,), (1,)), ((), ())), preferred_element_type=jnp.float32)


def over_rows(a, b):
    return lax.dot_general(a, b, (((0,), (0,)), ((), ())), preferred_element_type=jnp.float32)


def share_table(route_ids, gates, all_experts):
    named = route_ids[:, :, None] == jnp.arange(all_experts, dtype=jnp.int32)[None, None, :]
    return jnp.sum(jnp.where(named, gates[:, :, None], 0.0), axis=1)


def body(inputs, out_grad, expert_ids, gate_weights, w_gate, w_up, w_down):
    local_experts, hidden_share, model_width = w_gate.shape[1:]
    all_experts = local_experts * lax.axis_size("expert")
    units = local_experts * hidden_share
    gate_mat = w_gate[0].reshape(units, model_width)
    up_mat = w_up[0].reshape(units, model_width)
    down_mat = w_down[0].reshape(units, model_width)

    table = share_table(expert_ids[0], gate_weights[0], all_experts)
    table = lax.all_gather(table, GROUP, axis=0, tiled=True)
    tokens = lax.all_gather(inputs[0], GROUP, axis=0, tiled=True)
    grads_out = lax.all_gather(out_grad[0], GROUP, axis=0, tiled=True)
    own = lax.dynamic_slice_in_dim(
        table, lax.axis_index("expert") * local_experts, local_experts, axis=1
    )
    share = jnp.repeat(own, hidden_share, axis=1)

    pre_gate = rows_by(tokens, gate_mat)
    pre_up = rows_by(tokens, up_mat)
    sigmoid_gate = jax.nn.sigmoid(pre_gate)
    act_gate = pre_gate * sigmoid_gate
    hidden = (act_gate * pre_up * share).astype(jnp.bfloat16)
    hidden_grad = rows_by(grads_out, down_mat) * share
    gate_delta = (
        hidden_grad * pre_up * sigmoid_gate * (1.0 + pre_gate * (1.0 - sigmoid_gate))
    ).astype(jnp.bfloat16)
    up_delta = (hidden_grad * act_gate).astype(jnp.bfloat16)

    deltas = jnp.concatenate([gate_delta, up_delta], axis=1)
    mats = jnp.concatenate([gate_mat, up_mat], axis=0)
    partial_value = jnp.dot(deltas, mats, preferred_element_type=jnp.float32)
    token_grad = lax.psum_scatter(
        partial_value.astype(jnp.bfloat16), GROUP, scatter_dimension=0, tiled=True
    )
    grad_gate = over_rows(gate_delta, tokens).astype(jnp.bfloat16)
    grad_up = over_rows(up_delta, tokens).astype(jnp.bfloat16)
    grad_down = over_rows(hidden, grads_out).astype(jnp.bfloat16)
    grad_prev = passed_along(token_grad, "section", -1)
    shape = w_gate.shape
    return (
        grad_prev[None],
        grad_gate.reshape(shape),
        grad_up.reshape(shape),
        grad_down.reshape(shape),
    )


def solution(mesh):
    rows = P("section", GROUP, None)
    weights = P("section", "expert", "dp", None)
    return jax.shard_map(
        body,
        mesh=mesh,
        in_specs=(rows,) * 4 + (weights,) * 3,
        out_specs=(rows,) + (weights,) * 3,
        check_vma=False,
    )
```

```python
import functools

import jax
import jax.numpy as jnp
from jax import lax
from jax.experimental import pallas as pl
from jax.experimental.pallas import tpu as pltpu
from jax.sharding import PartitionSpec as P

GROUP = ("dp", "expert")


def passed_along(block, axis, distance):
    devices = range(lax.axis_size(axis))
    route = [(i - distance, i) for i in devices if i - distance in devices]
    return lax.ppermute(block, axis, route)


def rows_by(a, b):
    return lax.dot_general(a, b, (((1,), (1,)), ((), ())), preferred_element_type=jnp.float32)


def over_rows(a, b):
    return lax.dot_general(a, b, (((0,), (0,)), ((), ())), preferred_element_type=jnp.float32)


def share_table(route_ids, gates, all_experts):
    named = route_ids[:, :, None] == jnp.arange(all_experts, dtype=jnp.int32)[None, None, :]
    return jnp.sum(jnp.where(named, gates[:, :, None], 0.0), axis=1)


def gather_kernel(ways, lines, *refs):
    count = (len(refs) - 3) // 2
    own, full = refs[:count], refs[count : 2 * count]
    send_sem, recv_sem, local_sem = refs[2 * count :]
    dp, z = lax.axis_index("dp"), lax.axis_index("expert")
    across = lax.rem(dp + 2, lines)
    beside = dp + 1 - 2 * lax.rem(dp, 2)
    up, down = lax.rem(z + 1, ways), lax.rem(z + ways - 1, ways)

    def target(d, e):
        return {"dp": d, "expert": e}

    barrier = pltpu.get_barrier_semaphore()

    def greet(d, e):
        pl.semaphore_signal(
            barrier, inc=1, device_id=target(d, e), device_id_type=pl.DeviceIdType.MESH
        )

    greet(across, z)
    greet(beside, z)
    pl.when(z < ways - 1)(lambda: greet(dp, up))
    pl.when(z > 0)(lambda: greet(dp, down))
    inner = jnp.logical_and(z > 0, z < ways - 1)
    pl.when(inner)(lambda: pl.semaphore_wait(barrier, 4))
    pl.when(jnp.logical_not(inner))(lambda: pl.semaphore_wait(barrier, 3))

    def copy(i, line, place, number, d, e, from_own=False):
        slot = line * ways + place
        return pltpu.make_async_remote_copy(
            src_ref=own[i] if from_own else full[i].at[slot],
            dst_ref=full[i].at[slot],
            send_sem=send_sem.at[i, number],
            recv_sem=recv_sem.at[i, slot],
            device_id=target(d, e),
            device_id_type=pl.DeviceIdType.MESH,
        )

    everything = range(count)
    pending = []

    def send(cond, i, line, place, number, d, e, from_own=False):
        made = functools.partial(copy, i, line, place, number, d, e, from_own)
        if cond is None:
            made().start()
        else:
            pl.when(cond)(lambda: made().start())
        pending.append((cond, made))

    def received(i, line, place):
        copy(i, line, place, 0, across, z).wait_recv()

    steps = [(0, 0)] + [(j, sign) for j in range(1, ways) for sign in (-1, 1)]
    kept = [pltpu.make_async_copy(own[i], full[i].at[dp * ways + z], local_sem.at[i]) for i in everything]
    for i in everything:
        send(z < ways - 1, i, dp, z, 0, dp, up, True)
        send(z > 0, i, dp, z, ways, dp, down, True)
        send(None, i, dp, z, 2 * ways, across, z, True)
    for i in everything:
        send(None, i, dp, z, 4 * ways, beside, z, True)
        kept[i].start()
    wide = 2 * ways
    for n, (j, sign) in enumerate(steps):
        if n > 0:
            here = z >= j if sign < 0 else z + j < ways
            place = lax.rem(z + sign * j + ways, ways)
            number = n
            for i in everything:

                def arrive(i=i, place=place):
                    received(i, dp, place)

                pl.when(here)(arrive)
                if sign < 0:
                    if j < ways - 1:
                        send(jnp.logical_and(here, z < ways - 1), i, dp, place, j, dp, up)
                elif j < ways - 1:
                    send(jnp.logical_and(here, z > 0), i, dp, place, ways + j, dp, down)
                send(here, i, dp, place, wide + number, across, z)
                send(here, i, dp, place, 2 * wide + number, beside, z)
            cross_from(steps[n - 1], z, ways, everything, received, send, across, beside, 3 * wide + n - 1)
    cross_from(steps[-1], z, ways, everything, received, send, across, beside, 3 * wide + len(steps) - 1)
    other = lax.rem(beside + 2, lines)
    for line in (beside, other):
        for place in range(ways):
            for i in everything:
                received(i, line, place)
    for cond, made in pending:
        if cond is None:
            made().wait_send()
        else:
            pl.when(cond)(lambda made=made: made().wait_send())
    for k in kept:
        k.wait()


def cross_from(step, z, ways, everything, received, send, across, beside, number):
    j, sign = step
    here = None if j == 0 else (z >= j if sign < 0 else z + j < ways)
    place = lax.rem(z + sign * j + ways, ways)
    for i in everything:
        if here is None:
            received(i, across, place)
        else:
            pl.when(here)(lambda i=i: received(i, across, place))
        send(here, i, across, place, number, beside, z)


def gathered(*blocks):
    ways, lines = lax.axis_size("expert"), lax.axis_size("dp")
    slots = ways * lines
    full = pl.pallas_call(
        functools.partial(gather_kernel, ways, lines),
        out_shape=[jax.ShapeDtypeStruct((slots,) + b.shape, b.dtype) for b in blocks],
        in_specs=[pl.BlockSpec(memory_space=pl.ANY)] * len(blocks),
        out_specs=[pl.BlockSpec(memory_space=pl.ANY)] * len(blocks),
        scratch_shapes=[
            pltpu.SemaphoreType.DMA((len(blocks), 8 * ways)),
            pltpu.SemaphoreType.DMA((len(blocks), slots)),
            pltpu.SemaphoreType.DMA((len(blocks),)),
        ],
        compiler_params=pltpu.CompilerParams(collective_id=0, has_side_effects=True),
    )(*blocks)
    return [f.reshape((-1, f.shape[-1])) for f in full]


def body(inputs, out_grad, expert_ids, gate_weights, w_gate, w_up, w_down):
    local_experts, hidden_share, model_width = w_gate.shape[1:]
    all_experts = local_experts * lax.axis_size("expert")
    units = local_experts * hidden_share
    gate_mat = w_gate[0].reshape(units, model_width)
    up_mat = w_up[0].reshape(units, model_width)
    down_mat = w_down[0].reshape(units, model_width)

    table = share_table(expert_ids[0], gate_weights[0], all_experts)
    if (lax.axis_size("dp"), lax.axis_size("expert")) == (4, 4):
        table = jnp.pad(table, ((0, 0), (0, 128 - all_experts)))
        table, tokens, grads_out = gathered(table, inputs[0], out_grad[0])
    else:
        table, tokens, grads_out = (
            lax.all_gather(block, GROUP, axis=0, tiled=True)
            for block in (table, inputs[0], out_grad[0])
        )
    own = lax.dynamic_slice_in_dim(
        table, lax.axis_index("expert") * local_experts, local_experts, axis=1
    )
    share = jnp.repeat(own, hidden_share, axis=1)

    pre_gate = rows_by(tokens, gate_mat)
    pre_up = rows_by(tokens, up_mat)
    sigmoid_gate = jax.nn.sigmoid(pre_gate)
    act_gate = pre_gate * sigmoid_gate
    hidden = (act_gate * pre_up * share).astype(jnp.bfloat16)
    hidden_grad = rows_by(grads_out, down_mat) * share
    gate_delta = (
        hidden_grad * pre_up * sigmoid_gate * (1.0 + pre_gate * (1.0 - sigmoid_gate))
    ).astype(jnp.bfloat16)
    up_delta = (hidden_grad * act_gate).astype(jnp.bfloat16)

    deltas = jnp.concatenate([gate_delta, up_delta], axis=1)
    mats = jnp.concatenate([gate_mat, up_mat], axis=0)
    partial_value = jnp.dot(deltas, mats, preferred_element_type=jnp.float32)
    token_grad = lax.psum_scatter(
        partial_value.astype(jnp.bfloat16), GROUP, scatter_dimension=0, tiled=True
    )
    grad_gate = over_rows(gate_delta, tokens).astype(jnp.bfloat16)
    grad_up = over_rows(up_delta, tokens).astype(jnp.bfloat16)
    grad_down = over_rows(hidden, grads_out).astype(jnp.bfloat16)
    grad_prev = passed_along(token_grad, "section", -1)
    shape = w_gate.shape
    return (
        grad_prev[None],
        grad_gate.reshape(shape),
        grad_up.reshape(shape),
        grad_down.reshape(shape),
    )


def solution(mesh):
    rows = P("section", GROUP, None)
    weights = P("section", "expert", "dp", None)
    return jax.shard_map(
        body,
        mesh=mesh,
        in_specs=(rows,) * 4 + (weights,) * 3,
        out_specs=(rows,) + (weights,) * 3,
        check_vma=False,
    )
```

```python
import functools

import jax
import jax.numpy as jnp
from jax import lax
from jax.experimental import pallas as pl
from jax.experimental.pallas import tpu as pltpu
from jax.sharding import PartitionSpec as P

GROUP = ("dp", "expert")


def passed_along(block, axis, distance):
    devices = range(lax.axis_size(axis))
    route = [(i - distance, i) for i in devices if i - distance in devices]
    return lax.ppermute(block, axis, route)


def rows_by(a, b):
    return lax.dot_general(a, b, (((1,), (1,)), ((), ())), preferred_element_type=jnp.float32)


def over_rows(a, b):
    return lax.dot_general(a, b, (((0,), (0,)), ((), ())), preferred_element_type=jnp.float32)


def share_table(route_ids, gates, all_experts):
    named = route_ids[:, :, None] == jnp.arange(all_experts, dtype=jnp.int32)[None, None, :]
    return jnp.sum(jnp.where(named, gates[:, :, None], 0.0), axis=1)


def gather_kernel(ways, lines, *refs):
    count = (len(refs) - 3) // 2
    own, full = refs[:count], refs[count : 2 * count]
    pieces = pieces_of(own)
    send_sem, recv_sem, local_sem = refs[2 * count :]
    dp, z = lax.axis_index("dp"), lax.axis_index("expert")
    across = lax.rem(dp + 2, lines)
    beside = dp + 1 - 2 * lax.rem(dp, 2)
    up, down = lax.rem(z + 1, ways), lax.rem(z + ways - 1, ways)

    def target(d, e):
        return {"dp": d, "expert": e}

    barrier = pltpu.get_barrier_semaphore()

    def greet(d, e):
        pl.semaphore_signal(
            barrier, inc=1, device_id=target(d, e), device_id_type=pl.DeviceIdType.MESH
        )

    greet(across, z)
    greet(beside, z)
    pl.when(z < ways - 1)(lambda: greet(dp, up))
    pl.when(z > 0)(lambda: greet(dp, down))
    inner = jnp.logical_and(z > 0, z < ways - 1)
    pl.when(inner)(lambda: pl.semaphore_wait(barrier, 4))
    pl.when(jnp.logical_not(inner))(lambda: pl.semaphore_wait(barrier, 3))

    def copy(i, line, place, number, d, e, from_own=False):
        slot = line * ways + place
        which, start, rows, _ = pieces[i]
        span = pl.ds(start, rows)
        return pltpu.make_async_remote_copy(
            src_ref=own[which].at[span] if from_own else full[which].at[slot, span],
            dst_ref=full[which].at[slot, span],
            send_sem=send_sem.at[i, number],
            recv_sem=recv_sem.at[i, slot],
            device_id=target(d, e),
            device_id_type=pl.DeviceIdType.MESH,
        )

    everything = range(len(pieces))
    pending = []

    def send(cond, i, line, place, number, d, e, from_own=False):
        made = functools.partial(copy, i, line, place, number, d, e, from_own)
        if cond is None:
            made().start()
        else:
            pl.when(cond)(lambda: made().start())
        pending.append((cond, made))

    def received(i, line, place):
        copy(i, line, place, 0, across, z).wait_recv()

    steps = [(0, 0)] + [(j, sign) for j in range(1, ways) for sign in (-1, 1)]
    kept = [pltpu.make_async_copy(own[i], full[i].at[dp * ways + z], local_sem.at[i]) for i in range(count)]
    for i in everything:
        send(z < ways - 1, i, dp, z, 0, dp, up, True)
        send(z > 0, i, dp, z, ways, dp, down, True)
        send(None, i, dp, z, 2 * ways, across, z, True)
    for i in everything:
        send(None, i, dp, z, 4 * ways, beside, z, True)
    for k in kept:
        k.start()
    wide = 2 * ways
    for n, (j, sign) in enumerate(steps):
        if n > 0:
            here = z >= j if sign < 0 else z + j < ways
            place = lax.rem(z + sign * j + ways, ways)
            number = n
            for i in everything:

                def arrive(i=i, place=place):
                    received(i, dp, place)

                pl.when(here)(arrive)
                if sign < 0:
                    if j < ways - 1:
                        send(jnp.logical_and(here, z < ways - 1), i, dp, place, j, dp, up)
                elif j < ways - 1:
                    send(jnp.logical_and(here, z > 0), i, dp, place, ways + j, dp, down)
                if not pieces[i][3]:
                    send(here, i, dp, place, wide + number, across, z)
                send(here, i, dp, place, 2 * wide + number, beside, z)
            cross_from(steps[n - 1], z, ways, pieces, received, send, across, beside, dp, 3 * wide, n - 1)
    cross_from(steps[-1], z, ways, pieces, received, send, across, beside, dp, 3 * wide, len(steps) - 1)
    other = lax.rem(beside + 2, lines)
    for line in (beside, other):
        for place in range(ways):
            for i in everything:
                received(i, line, place)
    for cond, made in pending:
        if cond is None:
            made().wait_send()
        else:
            pl.when(cond)(lambda made=made: made().wait_send())
    for k in kept:
        k.wait()


def cross_from(step, z, ways, pieces, received, send, across, beside, dp, base, number):
    j, sign = step
    here = None if j == 0 else (z >= j if sign < 0 else z + j < ways)
    place = lax.rem(z + sign * j + ways, ways)
    for i, piece in enumerate(pieces):
        if here is None:
            received(i, across, place)
        else:
            pl.when(here)(lambda i=i: received(i, across, place))
        if piece[3] and j < ways - 1:
            sure = j == 0
            if sure or sign < 0:
                rising = z < ways - 1
                rising = rising if sure else jnp.logical_and(here, rising)
                send(rising, i, across, place, 2 * ways + 1 + j, dp, lax.rem(z + 1, ways))
            if sure or sign > 0:
                falling = z > 0
                falling = falling if sure else jnp.logical_and(here, falling)
                send(falling, i, across, place, 3 * ways + j, dp, lax.rem(z + ways - 1, ways))
        send(here, i, across, place, base + number, beside, z)


def pieces_of(blocks):
    pieces = []
    for i, block in enumerate(blocks):
        rows, early = block.shape[0], 16
        if i == 0 or rows <= early:
            pieces.append((i, 0, rows, False))
        else:
            pieces.append((i, 0, rows - early, False))
            pieces.append((i, rows - early, early, True))
    return pieces


def gathered(*blocks):
    ways, lines = lax.axis_size("expert"), lax.axis_size("dp")
    slots = ways * lines
    full = pl.pallas_call(
        functools.partial(gather_kernel, ways, lines),
        out_shape=[jax.ShapeDtypeStruct((slots,) + b.shape, b.dtype) for b in blocks],
        in_specs=[pl.BlockSpec(memory_space=pl.ANY)] * len(blocks),
        out_specs=[pl.BlockSpec(memory_space=pl.ANY)] * len(blocks),
        scratch_shapes=[
            pltpu.SemaphoreType.DMA((len(pieces_of(blocks)), 8 * ways)),
            pltpu.SemaphoreType.DMA((len(pieces_of(blocks)), slots)),
            pltpu.SemaphoreType.DMA((len(blocks),)),
        ],
        compiler_params=pltpu.CompilerParams(collective_id=0, has_side_effects=True),
    )(*blocks)
    return [f.reshape((-1, f.shape[-1])) for f in full]


def body(inputs, out_grad, expert_ids, gate_weights, w_gate, w_up, w_down):
    local_experts, hidden_share, model_width = w_gate.shape[1:]
    all_experts = local_experts * lax.axis_size("expert")
    units = local_experts * hidden_share
    gate_mat = w_gate[0].reshape(units, model_width)
    up_mat = w_up[0].reshape(units, model_width)
    down_mat = w_down[0].reshape(units, model_width)

    table = share_table(expert_ids[0], gate_weights[0], all_experts)
    if (lax.axis_size("dp"), lax.axis_size("expert")) == (4, 4):
        table = jnp.pad(table, ((0, 0), (0, 128 - all_experts)))
        table, tokens, grads_out = gathered(table, inputs[0], out_grad[0])
    else:
        table, tokens, grads_out = (
            lax.all_gather(block, GROUP, axis=0, tiled=True)
            for block in (table, inputs[0], out_grad[0])
        )
    own = lax.dynamic_slice_in_dim(
        table, lax.axis_index("expert") * local_experts, local_experts, axis=1
    )
    share = jnp.repeat(own, hidden_share, axis=1)

    pre_gate = rows_by(tokens, gate_mat)
    pre_up = rows_by(tokens, up_mat)
    sigmoid_gate = jax.nn.sigmoid(pre_gate)
    act_gate = pre_gate * sigmoid_gate
    hidden = (act_gate * pre_up * share).astype(jnp.bfloat16)
    hidden_grad = rows_by(grads_out, down_mat) * share
    gate_delta = (
        hidden_grad * pre_up * sigmoid_gate * (1.0 + pre_gate * (1.0 - sigmoid_gate))
    ).astype(jnp.bfloat16)
    up_delta = (hidden_grad * act_gate).astype(jnp.bfloat16)

    deltas = jnp.concatenate([gate_delta, up_delta], axis=1)
    mats = jnp.concatenate([gate_mat, up_mat], axis=0)
    partial_value = jnp.dot(deltas, mats, preferred_element_type=jnp.float32)
    token_grad = lax.psum_scatter(
        partial_value.astype(jnp.bfloat16), GROUP, scatter_dimension=0, tiled=True
    )
    grad_gate = over_rows(gate_delta, tokens).astype(jnp.bfloat16)
    grad_up = over_rows(up_delta, tokens).astype(jnp.bfloat16)
    grad_down = over_rows(hidden, grads_out).astype(jnp.bfloat16)
    grad_prev = passed_along(token_grad, "section", -1)
    shape = w_gate.shape
    return (
        grad_prev[None],
        grad_gate.reshape(shape),
        grad_up.reshape(shape),
        grad_down.reshape(shape),
    )


def solution(mesh):
    rows = P("section", GROUP, None)
    weights = P("section", "expert", "dp", None)
    return jax.shard_map(
        body,
        mesh=mesh,
        in_specs=(rows,) * 4 + (weights,) * 3,
        out_specs=(rows,) + (weights,) * 3,
        check_vma=False,
    )
```
